32 devices in a mesh: dp: 8 (over z, x), tensor: 4 (over y, core).
Axes of the slice: x: 2, y: 2, z: 4, core: 2. Of those that a mesh axis runs over, the one named last changes fastest.
Arguments:
- tokens: bfloat16 [4672, 768], P('dp'), may hold values from -6 to 6
- segment_ids: int32 [8, 584], P('dp'), may hold values from 0 to 2, never falling along the last dimension, each value on 1 to 511 neighbouring positions
- norm1_gain: float32 [2, 768], replicated, may hold values from 0.5 to 1.5
- norm1_shift: float32 [2, 768], replicated, may hold values from -1.75 to 1.75
- qkv_weight: bfloat16 [2, 768, 2304], P(None, None, 'tensor'), may hold values from -0.21875 to 0.21875
- qv_bias: float32 [2, 12, 128], P(None, 'tensor'), may hold values from -3 to 3
- out_weight: bfloat16 [2, 768, 768], P(None, 'tensor'), may hold values from -0.625 to 0.625
- out_bias: float32 [2, 768], replicated, may hold values from -1.75 to 1.75
- norm2_gain: float32 [2, 768], replicated, may hold values from 0.2 to 1.8
- norm2_shift: float32 [2, 768], replicated, may hold values from -1.75 to 1.75
- fc1_weight: bfloat16 [2, 768, 3072], P(None, None, 'tensor'), may hold values from -0.21875 to 0.21875
- fc1_bias: float32 [2, 3072], P(None, 'tensor'), may hold values from -3 to 3
- fc2_weight: bfloat16 [2, 3072, 768], P(None, 'tensor'), may hold values from -0.21875 to 0.21875
- fc2_bias: float32 [2, 768], replicated, may hold values from -3.5 to 3.5
- cotangent: bfloat16 [4672, 768], P('dp'), may hold values from -6 to 6
Outputs:
- output: float32 [4672, 768], P('dp')
- input_grad: float32 [4672, 768], P('dp')
- norm1_gain_grad: float32 [2, 768], P(None, 'dp')
- norm1_shift_grad: float32 [2, 768], P(None, 'dp')
- qkv_weight_grad: float32 [2, 768, 2304], P(None, 'dp', 'tensor')
- qv_bias_grad: float32 [2, 12, 128], P(None, 'tensor', 'dp')
- out_weight_grad: float32 [2, 768, 768], P(None, 'tensor', 'dp')
- out_bias_grad: float32 [2, 768], P(None, 'dp')
- norm2_gain_grad: float32 [2, 768], P(None, 'dp')
- norm2_shift_grad: float32 [2, 768], P(None, 'dp')
- fc1_weight_grad: float32 [2, 768, 3072], P(None, 'dp', 'tensor')
- fc1_bias_grad: float32 [2, 3072], P(None, ('tensor', 'dp'))
- fc2_weight_grad: float32 [2, 3072, 768], P(None, 'tensor', 'dp')
- fc2_bias_grad: float32 [2, 768], P(None, 'dp')
The draws below stay inside these ranges and needn't reach their ends.
Inputs may be any that keep to these rules, and one draw needn't show every extreme that they name: `segment_ids`: along each packed row the ids never fall; the tokens of a row with equal ids belong to one document.
All inputs are finite; a program needn't handle non-finite values.
Results may differ from the reference program's by a relative error of at most 0.028.
Values may be sent and summed in bfloat16 or wider, within the bound.
A program may use at most 128 MiB of HBM per device.

```python
import math
import jax
import jax.numpy as jnp
import numpy as np
from jax import lax

D = 768
HEADS = 12
HEAD_DIM = 64
FF = 3072
SEQ = 584
LAYERS = 2
ROWS = 8
TOKENS = 4672
N_TENSOR = 4


def block_scale(stream_key, dims, split, low, top_value):
    factor_of, own = 1.0, jax.random.fold_in(stream_key, 6)
    for axis_at, shards_of in split:
        heights = jnp.exp(jax.random.uniform(jax.random.fold_in(own, axis_at), (shards_of,), jnp.float32, low / len(split), top_value / len(split)))
        factor_of = factor_of * jnp.repeat(heights, dims[axis_at] // shards_of).reshape([-1 if axis == axis_at else 1 for axis in range(len(dims))])
    return factor_of


def split_up(count, total, most, slope):
    portions = [(1 << 20) // math.isqrt(rank ** slope) + 1 for rank in range(2, count + 1)]
    spare, counts = total - most - (count - 1), [1] * (count - 1)
    while spare > 0:
        movable = [i for i in range(count - 1) if counts[i] < most]
        mass, remaining = sum([portions[i] for i in movable]), spare
        for i in movable:
            more = min(most - counts[i], max(1, remaining * portions[i] // mass), spare)
            counts[i] = counts[i] + more
            spare = spare - more
    return np.array([most] + counts)


def uneven_parts(stream_key, count, total, reach, slope):
    if count == 2:
        one = jax.random.randint(stream_key, (), max(1, total - reach), min(reach, total - 1) + 1)
        return jnp.stack([one, total - one])
    lengths = jnp.asarray(split_up(count, total, reach, slope), jnp.int32)
    couples = (count - 1) // 2
    giver, sink = lengths[1:1 + 2 * couples:2], lengths[2:2 + 2 * couples:2]
    slack = jnp.minimum(giver - 1, reach - sink)
    shifted = jax.random.randint(jax.random.fold_in(stream_key, 1), (couples,), 0, 1 << 20) % (slack + 1)
    lengths = lengths.at[1:1 + 2 * couples:2].set(giver - shifted).at[2:2 + 2 * couples:2].set(sink + shifted)
    return lengths[jax.random.permutation(jax.random.fold_in(stream_key, 2), count)]


def gaussian(stream_key, extent, scale, most, pieces=(), dtype=jnp.bfloat16):
    factor_of = block_scale(stream_key, extent, pieces, -0.22, 0.18) if pieces else 1.0
    drawn = jax.random.normal(stream_key, extent, jnp.float32) * scale * factor_of
    return jnp.minimum(jnp.maximum(drawn, -most), most).astype(dtype)


def setup_inputs(seed: int = 0) -> dict:
    keys = jax.random.split(jax.random.key(seed), 16)
    return {
        "tokens": gaussian(keys[0], (TOKENS, D), 1.0, 6.0, ((0, 8),)),
        "segment_ids": jax.vmap(lambda own: jnp.searchsorted(jnp.cumsum(uneven_parts(own, 3, SEQ, SEQ - SEQ // 8, 0)), jnp.arange(SEQ), side="right"))(jax.random.split(keys[1], ROWS)).reshape((ROWS, SEQ)).astype(jnp.int32),
        "norm1_gain": jnp.clip(1.0 + 0.1 * jax.random.normal(keys[2], (LAYERS, D), jnp.float32), 0.5, 1.5),
        "norm1_shift": gaussian(keys[3], (LAYERS, D), 0.3, 1.75, (), jnp.float32),
        "qkv_weight": gaussian(keys[4], (LAYERS, D, 3 * D), D ** -0.5, 0.21875, ((2, 4),)),
        "qv_bias": gaussian(keys[5], (LAYERS, HEADS, 2 * HEAD_DIM), 0.5, 3.0, ((1, 4),), jnp.float32),
        "out_weight": gaussian(keys[6], (LAYERS, D, D), (D // 8) ** -0.5, 0.625, ((1, 4),)),
        "out_bias": gaussian(keys[7], (LAYERS, D), 0.3, 1.75, (), jnp.float32),
        "norm2_gain": jnp.clip(1.0 + 0.16 * jax.random.normal(keys[8], (LAYERS, D), jnp.float32), 0.2, 1.8),
        "norm2_shift": gaussian(keys[9], (LAYERS, D), 0.3, 1.75, (), jnp.float32),
        "fc1_weight": gaussian(keys[10], (LAYERS, D, FF), D ** -0.5, 0.21875, ((2, 4),)),
        "fc1_bias": gaussian(keys[11], (LAYERS, FF), 0.5, 3.0, ((1, 4),), jnp.float32),
        "fc2_weight": gaussian(keys[12], (LAYERS, FF, D), (FF // 4) ** -0.5, 0.21875, ((1, 4),)),
        "fc2_bias": gaussian(keys[13], (LAYERS, D), 0.6, 3.5, (), jnp.float32),
        "cotangent": gaussian(keys[14], (TOKENS, D), 1.0, 6.0, ((0, 8),)),
    }


NORM_EPS = 1e-05
GELU_C = 0.7978845608028654
NEG_FILL = -1e+30

def layer_norm(hidden, norm_gain, norm_shift):
    row_mean = lax.optimization_barrier(jnp.mean(hidden, axis=-1, keepdims=True))
    centred = hidden - row_mean
    variance = lax.optimization_barrier(jnp.mean(centred * centred, axis=-1, keepdims=True))
    inverse = lax.rsqrt(variance + NORM_EPS)
    normal = centred * inverse
    return (normal * norm_gain + norm_shift, normal, inverse)

def norm_backward(grad_out, normal, inverse, norm_gain):
    scaled = grad_out * norm_gain
    return inverse * (scaled - lax.optimization_barrier(jnp.mean(scaled, axis=-1, keepdims=True)) - normal * lax.optimization_barrier(jnp.mean(scaled * normal, axis=-1, keepdims=True)))

def gelu_pair(preact):
    inner_arg = GELU_C * (preact + 0.044715 * preact * preact * preact)
    tanh_value = jnp.tanh(inner_arg)
    gelu_out = 0.5 * preact * (1.0 + tanh_value)
    gelu_slope = 0.5 * (1.0 + tanh_value) + 0.5 * preact * (1.0 - tanh_value * tanh_value) * GELU_C * (1.0 + 3.0 * 0.044715 * preact * preact)
    return (gelu_out, gelu_slope)

def group_total(left_mat, right_mat):
    row_count = left_mat.shape[0]
    inner_width = left_mat.shape[1] // N_TENSOR
    left_parts = left_mat.reshape(row_count, N_TENSOR, inner_width).astype(jnp.float32)
    right_parts = right_mat.reshape(N_TENSOR, inner_width, right_mat.shape[1]).astype(jnp.float32)
    partials = jnp.einsum('ngk,gkd->gnd', left_parts, right_parts)
    rounded = lax.optimization_barrier(partials.astype(jnp.bfloat16))
    return lax.optimization_barrier(jnp.sum(rounded.astype(jnp.float32), axis=0))

def attend_scores(queries, key_vecs, allowed):
    score_scale = queries.shape[-1] ** (-0.5)
    scores = jnp.einsum('rqhd,rkhd->rhqk', queries.astype(jnp.float32), key_vecs.astype(jnp.float32)) * score_scale
    return jnp.where(allowed, scores, NEG_FILL)

def forward_layer(hidden, allowed, params):
    gain_one, shift_one, qkv_w, qv_b, out_w, out_b, gain_two, shift_two, up_w, up_b, down_w, down_b = params
    tok_count = hidden.shape[0]
    head_count = qv_b.shape[0]
    head_size = qv_b.shape[1] // 2
    normed, normal_one, inverse_one = layer_norm(hidden, gain_one, shift_one)
    normed_b = normed.astype(jnp.bfloat16)
    projected = jnp.dot(normed_b, qkv_w, preferred_element_type=jnp.float32)
    projected = projected.reshape(1, tok_count, head_count, 3, head_size)
    queries = (projected[:, :, :, 0] + qv_b[:, :head_size]).astype(jnp.bfloat16)
    key_vecs = projected[:, :, :, 1].astype(jnp.bfloat16)
    values = (projected[:, :, :, 2] + qv_b[:, head_size:]).astype(jnp.bfloat16)
    scores = attend_scores(queries, key_vecs, allowed)
    row_top = lax.optimization_barrier(jnp.max(scores, axis=-1, keepdims=True))
    log_total = row_top + jnp.log(lax.optimization_barrier(jnp.sum(jnp.exp(scores - row_top), axis=-1, keepdims=True)))
    weights = jnp.exp(scores - log_total).astype(jnp.bfloat16)
    mixed_heads = jnp.einsum('rhqk,rkhd->rqhd', weights.astype(jnp.float32), values.astype(jnp.float32))
    mixed_heads = mixed_heads.astype(jnp.bfloat16).reshape(tok_count, head_count * head_size)
    after_attn = hidden + group_total(mixed_heads, out_w) + out_b
    middle, normal_two, inverse_two = layer_norm(after_attn, gain_two, shift_two)
    mid_b = middle.astype(jnp.bfloat16)
    preact = jnp.dot(mid_b, up_w, preferred_element_type=jnp.float32) + up_b
    gelu_out, gelu_slope = gelu_pair(preact)
    gelu_b = gelu_out.astype(jnp.bfloat16)
    block_out = after_attn + group_total(gelu_b, down_w) + down_b
    saved = (normed_b, normal_one, inverse_one, queries, key_vecs, values, log_total, mixed_heads, normal_two, inverse_two, mid_b, gelu_slope, gelu_b)
    return (block_out, saved)

def backward_layer(grad_out, allowed, params, saved):
    gain_one, shift_one, qkv_w, qv_b, out_w, out_b, gain_two, shift_two, up_w, up_b, down_w, down_b = params
    normed_b, normal_one, inverse_one, queries, key_vecs, values, log_total, mixed_heads, normal_two, inverse_two, mid_b, gelu_slope, gelu_b = saved
    tok_count = grad_out.shape[0]
    head_count = qv_b.shape[0]
    head_size = qv_b.shape[1] // 2
    score_scale = head_size ** (-0.5)
    down_b_grad = lax.optimization_barrier(jnp.sum(grad_out, axis=0))
    grad_out_b = grad_out.astype(jnp.bfloat16)
    down_w_grad = jnp.dot(gelu_b.T, grad_out_b, preferred_element_type=jnp.float32)
    gelu_grad = jnp.dot(grad_out_b, down_w.T, preferred_element_type=jnp.float32)
    pre_grad = gelu_grad * gelu_slope
    up_b_grad = lax.optimization_barrier(jnp.sum(pre_grad, axis=0))
    pre_grad_b = pre_grad.astype(jnp.bfloat16)
    up_w_grad = jnp.dot(mid_b.T, pre_grad_b, preferred_element_type=jnp.float32)
    mid_grad = group_total(pre_grad_b, up_w.T)
    gain_two_grad = lax.optimization_barrier(jnp.sum(mid_grad * normal_two, axis=0))
    shift_two_grad = lax.optimization_barrier(jnp.sum(mid_grad, axis=0))
    resid_grad = grad_out + norm_backward(mid_grad, normal_two, inverse_two, gain_two)
    out_b_grad = lax.optimization_barrier(jnp.sum(resid_grad, axis=0))
    resid_b = resid_grad.astype(jnp.bfloat16)
    out_w_grad = jnp.dot(mixed_heads.T, resid_b, preferred_element_type=jnp.float32)
    heads_grad = jnp.dot(resid_b, out_w.T, preferred_element_type=jnp.float32).astype(jnp.bfloat16)
    heads_grad = heads_grad.reshape(1, tok_count, head_count, head_size)
    scores = attend_scores(queries, key_vecs, allowed)
    probs = jnp.exp(scores - log_total)
    probs_b = probs.astype(jnp.bfloat16)
    prob_grad = jnp.einsum('rqhd,rkhd->rhqk', heads_grad.astype(jnp.float32), values.astype(jnp.float32))
    mixed_four = mixed_heads.reshape(1, tok_count, head_count, head_size)
    row_dots = lax.optimization_barrier(jnp.sum(heads_grad.astype(jnp.float32) * mixed_four.astype(jnp.float32), axis=-1))
    row_dots = jnp.transpose(row_dots, (0, 2, 1))[..., None]
    score_grad = (probs * (prob_grad - row_dots) * score_scale).astype(jnp.bfloat16)
    query_grad = jnp.einsum('rhqk,rkhd->rqhd', score_grad.astype(jnp.float32), key_vecs.astype(jnp.float32))
    key_grad = jnp.einsum('rhqk,rqhd->rkhd', score_grad.astype(jnp.float32), queries.astype(jnp.float32))
    value_grad = jnp.einsum('rhqk,rqhd->rkhd', probs_b.astype(jnp.float32), heads_grad.astype(jnp.float32))
    qv_b_grad = jnp.concatenate([lax.optimization_barrier(jnp.sum(query_grad, axis=(0, 1))), lax.optimization_barrier(jnp.sum(value_grad, axis=(0, 1)))], axis=-1)
    proj_grad = jnp.stack([query_grad, key_grad, value_grad], axis=3).astype(jnp.bfloat16)
    proj_grad = proj_grad.reshape(tok_count, head_count * 3 * head_size)
    qkv_w_grad = jnp.dot(normed_b.T, proj_grad, preferred_element_type=jnp.float32)
    normed_grad = group_total(proj_grad, qkv_w.T)
    gain_one_grad = lax.optimization_barrier(jnp.sum(normed_grad * normal_one, axis=0))
    shift_one_grad = lax.optimization_barrier(jnp.sum(normed_grad, axis=0))
    input_grad = resid_grad + norm_backward(normed_grad, normal_one, inverse_one, gain_one)
    grads = (gain_one_grad, shift_one_grad, qkv_w_grad, qv_b_grad, out_w_grad, out_b_grad, gain_two_grad, shift_two_grad, up_w_grad, up_b_grad, down_w_grad, down_b_grad)
    return (input_grad, grads)

def row_pass(token_row, segment_row, cot_row, stacked):
    seq_len = segment_row.shape[0]
    same_doc = segment_row[:, None] == segment_row[None, :]
    positions = lax.broadcasted_iota(jnp.int32, (seq_len, seq_len), 0)
    earlier = lax.broadcasted_iota(jnp.int32, (seq_len, seq_len), 1) <= positions
    allowed = (same_doc & earlier)[None, None]
    hidden = token_row.astype(jnp.float32)
    saved_list = []
    for layer_idx in range(LAYERS):
        params = tuple((member[layer_idx] for member in stacked))
        hidden, saved = forward_layer(hidden, allowed, params)
        saved_list.append(saved)
    grad_flow = cot_row.astype(jnp.float32)
    per_layer = [None] * LAYERS
    for layer_idx in reversed(range(LAYERS)):
        params = tuple((member[layer_idx] for member in stacked))
        grad_flow, grads = backward_layer(grad_flow, allowed, params, saved_list[layer_idx])
        per_layer[layer_idx] = grads
    stacked_grads = tuple((jnp.stack([layer_grads[position] for layer_grads in per_layer], axis=0) for position in range(12)))
    return (hidden, grad_flow, stacked_grads)

def reference(tokens, segment_ids, norm1_gain, norm1_shift, qkv_weight, qv_bias, out_weight, out_bias, norm2_gain, norm2_shift, fc1_weight, fc1_bias, fc2_weight, fc2_bias, cotangent):
    stacked = (norm1_gain, norm1_shift, qkv_weight, qv_bias, out_weight, out_bias, norm2_gain, norm2_shift, fc1_weight, fc1_bias, fc2_weight, fc2_bias)
    token_rows = tokens.reshape(ROWS, SEQ, D)
    cot_rows = cotangent.reshape(ROWS, SEQ, D)

    def row_step(totals, row_inputs):
        token_row, segment_row, cot_row = row_inputs
        out_row, grad_row, grads = row_pass(token_row, segment_row, cot_row, stacked)
        return (jax.tree.map(jnp.add, totals, grads), (out_row, grad_row))
    start = tuple((jnp.zeros(member.shape, jnp.float32) for member in stacked))
    totals, (out_rows, grad_rows) = lax.scan(row_step, start, (token_rows, segment_ids, cot_rows))
    grad_scale = float(TOKENS) ** (-0.5)
    totals = tuple((member * grad_scale for member in totals))
    output = out_rows.reshape(TOKENS, D)
    input_grad = grad_rows.reshape(TOKENS, D)
    return (output, input_grad, totals[0], totals[1], totals[2], totals[3], totals[4], totals[5], totals[6], totals[7], totals[8], totals[9], totals[10], totals[11])
```

```python
import functools

import jax
import jax.numpy as jnp
from jax import lax
from jax.experimental import pallas as pl
from jax.experimental.pallas import tpu as pltpu
from jax.sharding import PartitionSpec as P

NORM_EPS = 1e-05
GELU_C = 0.7978845608028654
NEG_FILL = -1e30


def layer_norm(hidden, norm_gain, norm_shift):
    row_mean = jnp.mean(hidden, axis=-1, keepdims=True)
    centred = hidden - row_mean
    variance = jnp.mean(centred * centred, axis=-1, keepdims=True)
    inverse = lax.rsqrt(variance + NORM_EPS)
    normal = centred * inverse
    return (normal * norm_gain + norm_shift, normal, inverse)


def norm_backward(grad_out, normal, inverse, norm_gain):
    scaled = grad_out * norm_gain
    return inverse * (
        scaled
        - jnp.mean(scaled, axis=-1, keepdims=True)
        - normal * jnp.mean(scaled * normal, axis=-1, keepdims=True)
    )


def gelu_pair(preact):
    inner_arg = GELU_C * (preact + 0.044715 * preact * preact * preact)
    tanh_value = jnp.tanh(inner_arg)
    gelu_out = 0.5 * preact * (1.0 + tanh_value)
    gelu_slope = 0.5 * (1.0 + tanh_value) + 0.5 * preact * (
        1.0 - tanh_value * tanh_value
    ) * GELU_C * (1.0 + 3.0 * 0.044715 * preact * preact)
    return (gelu_out, gelu_slope)


MESH = pl.DeviceIdType.MESH
CHUNK = 128


def total_kernel(transposed, x_ref, w_ref, out_ref, own, near_out, near_in, far_out, far_in,
                 near_send, near_recv, far_send, far_recv, back_send, back_recv):
    here = lax.axis_index("tensor")
    core = lax.rem(here, 2)
    near = here + 1 - 2 * core
    far = lax.rem(here + 2, 4)
    barrier = pltpu.get_barrier_semaphore()
    for other in (near, far):
        pl.semaphore_signal(barrier, inc=1, device_id={"tensor": other}, device_id_type=MESH)

    half = out_ref.shape[1] // 2
    count = half // CHUNK

    def part(side, j):
        start = pl.multiple_of(side * half + j * CHUNK, CHUNK)
        if transposed:
            return lax.dot_general(
                x_ref[...], w_ref[pl.ds(start, CHUNK), :], (((1,), (1,)), ((), ())),
                preferred_element_type=jnp.float32,
            )
        return jnp.dot(x_ref[...], w_ref[:, pl.ds(start, CHUNK)], preferred_element_type=jnp.float32)

    def copy(src, dst, send, recv, other):
        return pltpu.make_async_remote_copy(
            src_ref=src, dst_ref=dst, send_sem=send, recv_sem=recv,
            device_id={"tensor": other}, device_id_type=MESH,
        )

    first = [copy(near_out.at[j], near_in.at[j], near_send.at[j], near_recv.at[j], near) for j in range(count)]
    second = [copy(far_out.at[j], far_in.at[j], far_send.at[j], far_recv.at[j], far) for j in range(count)]

    def back_copy(j):
        columns = pl.ds(pl.multiple_of(core * half + j * CHUNK, CHUNK), CHUNK)
        return copy(out_ref.at[:, columns], out_ref.at[:, columns], back_send.at[j], back_recv.at[j], near)

    third = [back_copy(j) for j in range(count)]

    near_out[0] = part(1 - core, 0).astype(jnp.bfloat16)
    pl.semaphore_wait(barrier, 2)
    first[0].start()
    own[0] = part(core, 0)
    for j in range(count):
        if j + 1 < count:
            near_out[j + 1] = part(1 - core, j + 1).astype(jnp.bfloat16)
            first[j + 1].start()
            own[j + 1] = part(core, j + 1)
        first[j].wait_recv()
        far_out[j] = (own[j] + near_in[j].astype(jnp.float32)).astype(jnp.bfloat16)
        second[j].start()
    for j in range(count):
        second[j].wait_recv()
        columns = pl.ds(pl.multiple_of(core * half + j * CHUNK, CHUNK), CHUNK)
        out_ref[:, columns] = (
            far_out[j].astype(jnp.float32) + far_in[j].astype(jnp.float32)
        ).astype(jnp.bfloat16)
        third[j].start()
    for j in range(count):
        first[j].wait_send()
        second[j].wait_send()
        third[j].wait()


def group_total(x, w, transposed, collective_id):
    rows = x.shape[0]
    columns = w.shape[0] if transposed else w.shape[1]
    count = columns // 2 // CHUNK
    vmem = pl.BlockSpec(memory_space=pltpu.VMEM)
    slot = pltpu.VMEM((count, rows, CHUNK), jnp.bfloat16)
    return pl.pallas_call(
        functools.partial(total_kernel, transposed),
        out_shape=jax.ShapeDtypeStruct((rows, columns), jnp.bfloat16),
        in_specs=[vmem, vmem],
        out_specs=vmem,
        scratch_shapes=[pltpu.VMEM((count, rows, CHUNK), jnp.float32), slot, slot, slot, slot]
        + [pltpu.SemaphoreType.DMA((count,))] * 6,
        compiler_params=pltpu.CompilerParams(
            collective_id=collective_id, has_side_effects=True, vmem_limit_bytes=32 * 2**20
        ),
        cost_estimate=pl.CostEstimate(
            flops=2 * rows * columns * x.shape[1], bytes_accessed=rows * columns * 8, transcendentals=0
        ),
    )(x, w).astype(jnp.float32)


def spread(grad, dimension):
    return lax.psum_scatter(
        grad.astype(jnp.bfloat16), "dp", scatter_dimension=dimension, tiled=True
    ).astype(jnp.float32)


SPLIT = (0, 0, 0, 1, 1, 0, 0, 0, 0, 0, 1, 0)


def sum_layer(grads):
    return tuple(spread(g, d) if g.ndim > 1 and g.shape[0] > 8 else
                 lax.psum_scatter(g, "dp", scatter_dimension=d, tiled=True) for g, d in zip(grads, SPLIT))


def attend_scores(queries, key_vecs, allowed):
    score_scale = queries.shape[-1] ** (-0.5)
    scores = (
        jnp.einsum("rqhd,rkhd->rhqk", queries, key_vecs, preferred_element_type=jnp.float32)
        * score_scale
    )
    return jnp.where(allowed, scores, NEG_FILL)


def forward_layer(hidden, allowed, params, batch_rows):
    (
        gain_one,
        shift_one,
        qkv_w,
        qv_b,
        out_w,
        out_b,
        gain_two,
        shift_two,
        up_w,
        up_b,
        down_w,
        down_b,
    ) = params
    tok_count = hidden.shape[0]
    local_heads = qv_b.shape[0]
    head_size = qv_b.shape[1] // 2
    normed, normal_one, inverse_one = layer_norm(hidden, gain_one, shift_one)
    normed_b = normed.astype(jnp.bfloat16)
    projected = jnp.dot(normed_b, qkv_w, preferred_element_type=jnp.float32)
    projected = projected.reshape(batch_rows, tok_count // batch_rows, local_heads, 3, head_size)
    queries = (projected[:, :, :, 0] + qv_b[:, :head_size]).astype(jnp.bfloat16)
    key_vecs = projected[:, :, :, 1].astype(jnp.bfloat16)
    values = (projected[:, :, :, 2] + qv_b[:, head_size:]).astype(jnp.bfloat16)
    scores = attend_scores(queries, key_vecs, allowed)
    row_top = jnp.max(scores, axis=-1, keepdims=True)
    log_total = row_top + jnp.log(jnp.sum(jnp.exp(scores - row_top), axis=-1, keepdims=True))
    weights = jnp.exp(scores - log_total).astype(jnp.bfloat16)
    mixed_heads = jnp.einsum("rhqk,rkhd->rqhd", weights, values, preferred_element_type=jnp.float32)
    mixed_heads = mixed_heads.astype(jnp.bfloat16).reshape(tok_count, local_heads * head_size)
    after_attn = (
        hidden
        + group_total(mixed_heads, out_w, False, 0)
        + out_b
    )
    middle, normal_two, inverse_two = layer_norm(after_attn, gain_two, shift_two)
    mid_b = middle.astype(jnp.bfloat16)
    preact = jnp.dot(mid_b, up_w, preferred_element_type=jnp.float32) + up_b
    gelu_out, gelu_slope = gelu_pair(preact)
    gelu_b = gelu_out.astype(jnp.bfloat16)
    block_out = (
        after_attn
        + group_total(gelu_b, down_w, False, 1)
        + down_b
    )
    saved = (
        normed_b,
        normal_one,
        inverse_one,
        queries,
        key_vecs,
        values,
        log_total,
        mixed_heads,
        normal_two,
        inverse_two,
        mid_b,
        gelu_slope,
        gelu_b,
    )
    return (block_out, saved)


def backward_layer(grad_out, allowed, params, saved, batch_rows):
    (
        gain_one,
        shift_one,
        qkv_w,
        qv_b,
        out_w,
        out_b,
        gain_two,
        shift_two,
        up_w,
        up_b,
        down_w,
        down_b,
    ) = params
    (
        normed_b,
        normal_one,
        inverse_one,
        queries,
        key_vecs,
        values,
        log_total,
        mixed_heads,
        normal_two,
        inverse_two,
        mid_b,
        gelu_slope,
        gelu_b,
    ) = saved
    tok_count = grad_out.shape[0]
    local_heads = qv_b.shape[0]
    head_size = qv_b.shape[1] // 2
    score_scale = head_size ** (-0.5)
    down_b_grad = jnp.sum(grad_out, axis=0)
    grad_out_b = grad_out.astype(jnp.bfloat16)
    down_w_grad = jnp.einsum("nf,nd->fd", gelu_b, grad_out_b, preferred_element_type=jnp.float32)
    gelu_grad = jnp.einsum("nd,fd->nf", grad_out_b, down_w, preferred_element_type=jnp.float32)
    pre_grad = gelu_grad * gelu_slope
    up_b_grad = jnp.sum(pre_grad, axis=0)
    pre_grad_b = pre_grad.astype(jnp.bfloat16)
    up_w_grad = jnp.einsum("nd,nf->df", mid_b, pre_grad_b, preferred_element_type=jnp.float32)
    mid_grad = group_total(pre_grad_b, up_w, True, 2)
    gain_two_grad = jnp.sum(mid_grad * normal_two, axis=0)
    shift_two_grad = jnp.sum(mid_grad, axis=0)
    resid_grad = grad_out + norm_backward(mid_grad, normal_two, inverse_two, gain_two)
    out_b_grad = jnp.sum(resid_grad, axis=0)
    resid_b = resid_grad.astype(jnp.bfloat16)
    out_w_grad = jnp.einsum("nk,nd->kd", mixed_heads, resid_b, preferred_element_type=jnp.float32)
    heads_grad = jnp.einsum("nd,kd->nk", resid_b, out_w, preferred_element_type=jnp.float32).astype(
        jnp.bfloat16
    )
    heads_grad = heads_grad.reshape(batch_rows, tok_count // batch_rows, local_heads, head_size)
    scores = attend_scores(queries, key_vecs, allowed)
    probs = jnp.exp(scores - log_total)
    probs_b = probs.astype(jnp.bfloat16)
    prob_grad = jnp.einsum(
        "rqhd,rkhd->rhqk", heads_grad, values, preferred_element_type=jnp.float32
    )
    mixed_four = mixed_heads.reshape(batch_rows, tok_count // batch_rows, local_heads, head_size)
    row_dots = jnp.sum(heads_grad.astype(jnp.float32) * mixed_four.astype(jnp.float32), axis=-1)
    row_dots = jnp.transpose(row_dots, (0, 2, 1))[..., None]
    score_grad = (probs * (prob_grad - row_dots) * score_scale).astype(jnp.bfloat16)
    query_grad = jnp.einsum(
        "rhqk,rkhd->rqhd", score_grad, key_vecs, preferred_element_type=jnp.float32
    )
    key_grad = jnp.einsum(
        "rhqk,rqhd->rkhd", score_grad, queries, preferred_element_type=jnp.float32
    )
    value_grad = jnp.einsum(
        "rhqk,rqhd->rkhd", probs_b, heads_grad, preferred_element_type=jnp.float32
    )
    qv_b_grad = jnp.concatenate(
        [jnp.sum(query_grad, axis=(0, 1)), jnp.sum(value_grad, axis=(0, 1))], axis=-1
    )
    proj_grad = jnp.stack([query_grad, key_grad, value_grad], axis=3).astype(jnp.bfloat16)
    proj_grad = proj_grad.reshape(tok_count, local_heads * 3 * head_size)
    qkv_w_grad = jnp.einsum("nd,nc->dc", normed_b, proj_grad, preferred_element_type=jnp.float32)
    normed_grad = group_total(proj_grad, qkv_w, True, 3)
    gain_one_grad = jnp.sum(normed_grad * normal_one, axis=0)
    shift_one_grad = jnp.sum(normed_grad, axis=0)
    input_grad = resid_grad + norm_backward(normed_grad, normal_one, inverse_one, gain_one)
    grads = (
        gain_one_grad,
        shift_one_grad,
        qkv_w_grad,
        qv_b_grad,
        out_w_grad,
        out_b_grad,
        gain_two_grad,
        shift_two_grad,
        up_w_grad,
        up_b_grad,
        down_w_grad,
        down_b_grad,
    )
    return (input_grad, grads)


def body(
    tokens,
    segment_ids,
    norm1_gain,
    norm1_shift,
    qkv_weight,
    qv_bias,
    out_weight,
    out_bias,
    norm2_gain,
    norm2_shift,
    fc1_weight,
    fc1_bias,
    fc2_weight,
    fc2_bias,
    cotangent,
):
    stacked = (
        norm1_gain,
        norm1_shift,
        qkv_weight,
        qv_bias,
        out_weight,
        out_bias,
        norm2_gain,
        norm2_shift,
        fc1_weight,
        fc1_bias,
        fc2_weight,
        fc2_bias,
    )
    batch_rows, seq_len = segment_ids.shape
    layer_count = norm1_gain.shape[0]
    grad_scale = float(batch_rows * seq_len * lax.axis_size("dp")) ** (-0.5)
    padded = -(-seq_len // 16) * 16
    extra = padded - seq_len
    segment_ids = jnp.pad(segment_ids, ((0, 0), (0, extra)), constant_values=-1)
    same_doc = segment_ids[:, :, None] == segment_ids[:, None, :]
    positions = lax.broadcasted_iota(jnp.int32, (padded, padded), 0)
    earlier = lax.broadcasted_iota(jnp.int32, (padded, padded), 1) <= positions
    allowed = (same_doc & earlier[None])[:, None]

    def widen(rows):
        rows = rows.astype(jnp.float32).reshape(batch_rows, seq_len, -1)
        return jnp.pad(rows, ((0, 0), (0, extra), (0, 0))).reshape(batch_rows * padded, -1)

    def narrow(rows):
        return rows.reshape(batch_rows, padded, -1)[:, :seq_len].reshape(batch_rows * seq_len, -1)

    hidden = widen(tokens)
    saved_list = []
    for layer_idx in range(layer_count):
        params = tuple((member[layer_idx] for member in stacked))
        hidden, saved = forward_layer(hidden, allowed, params, batch_rows)
        saved_list.append(saved)
    grad_flow = widen(cotangent)
    per_layer = [None] * layer_count
    for layer_idx in reversed(range(layer_count)):
        params = tuple((member[layer_idx] for member in stacked))
        grad_flow, grads = backward_layer(
            grad_flow, allowed, params, saved_list[layer_idx], batch_rows
        )
        per_layer[layer_idx] = sum_layer(grads)
    totals = tuple(
        jnp.stack([part[i] for part in per_layer], axis=0) * grad_scale for i in range(12)
    )
    return (narrow(hidden), narrow(grad_flow)) + totals


def solution(mesh):
    return jax.shard_map(
        body,
        mesh=mesh,
        in_specs=(
            P("dp", None),
            P("dp", None),
            P(),
            P(),
            P(None, None, "tensor"),
            P(None, "tensor", None),
            P(None, "tensor", None),
            P(),
            P(),
            P(),
            P(None, None, "tensor"),
            P(None, "tensor"),
            P(None, "tensor", None),
            P(),
            P("dp", None),
        ),
        out_specs=(
            P("dp", None),
            P("dp", None),
            P(None, "dp"),
            P(None, "dp"),
            P(None, "dp", "tensor"),
            P(None, "tensor", "dp"),
            P(None, "tensor", "dp"),
            P(None, "dp"),
            P(None, "dp"),
            P(None, "dp"),
            P(None, "dp", "tensor"),
            P(None, ("tensor", "dp")),
            P(None, "tensor", "dp"),
            P(None, "dp"),
        ),
        check_vma=False,
    )
```

```python
import functools

import jax
import jax.numpy as jnp
from jax import lax
from jax.experimental import pallas as pl
from jax.experimental.pallas import tpu as pltpu
from jax.sharding import PartitionSpec as P

NORM_EPS = 1e-05
GELU_C = 0.7978845608028654
NEG_FILL = -1e30


def layer_norm(hidden, norm_gain, norm_shift):
    row_mean = jnp.mean(hidden, axis=-1, keepdims=True)
    centred = hidden - row_mean
    variance = jnp.mean(centred * centred, axis=-1, keepdims=True)
    inverse = lax.rsqrt(variance + NORM_EPS)
    normal = centred * inverse
    return (normal * norm_gain + norm_shift, normal, inverse)


def norm_backward(grad_out, normal, inverse, norm_gain):
    scaled = grad_out * norm_gain
    return inverse * (
        scaled
        - jnp.mean(scaled, axis=-1, keepdims=True)
        - normal * jnp.mean(scaled * normal, axis=-1, keepdims=True)
    )


def gelu_pair(preact):
    inner_arg = GELU_C * (preact + 0.044715 * preact * preact * preact)
    tanh_value = jnp.tanh(inner_arg)
    gelu_out = 0.5 * preact * (1.0 + tanh_value)
    gelu_slope = 0.5 * (1.0 + tanh_value) + 0.5 * preact * (
        1.0 - tanh_value * tanh_value
    ) * GELU_C * (1.0 + 3.0 * 0.044715 * preact * preact)
    return (gelu_out, gelu_slope)


MESH = pl.DeviceIdType.MESH
CHUNK = 128


def total_kernel(transposed, x_ref, w_ref, out_ref, own, near_out, near_in, far_out, far_in,
                 near_send, near_recv, far_send, far_recv, back_send, back_recv, extra=0, beside=None):
    here = lax.axis_index("tensor")
    core = lax.rem(here, 2)
    near = here + 1 - 2 * core
    far = lax.rem(here + 2, 4)
    barrier = pltpu.get_barrier_semaphore()
    for other in (near, far):
        pl.semaphore_signal(barrier, inc=1, device_id={"tensor": other}, device_id_type=MESH)

    half = out_ref.shape[1] // 2
    count = half // CHUNK

    def part(side, j):
        start = pl.multiple_of(side * half + j * CHUNK, CHUNK)
        if transposed:
            return lax.dot_general(
                x_ref[...], w_ref[pl.ds(start, CHUNK), :], (((1,), (1,)), ((), ())),
                preferred_element_type=jnp.float32,
            )
        return jnp.dot(x_ref[...], w_ref[:, pl.ds(start, CHUNK)], preferred_element_type=jnp.float32)

    def copy(src, dst, send, recv, other):
        return pltpu.make_async_remote_copy(
            src_ref=src, dst_ref=dst, send_sem=send, recv_sem=recv,
            device_id={"tensor": other}, device_id_type=MESH,
        )

    first = [copy(near_out.at[j], near_in.at[j], near_send.at[j], near_recv.at[j], near) for j in range(count)]
    second = [copy(far_out.at[j], far_in.at[j], far_send.at[j], far_recv.at[j], far) for j in range(count)]

    def back_copy(j):
        columns = pl.ds(pl.multiple_of(core * half + j * CHUNK, CHUNK), CHUNK)
        return copy(out_ref.at[:, columns], out_ref.at[:, columns], back_send.at[j], back_recv.at[j], near)

    third = [back_copy(j) for j in range(count)]

    near_out[0] = part(1 - core, 0).astype(jnp.bfloat16)
    pl.semaphore_wait(barrier, 2 + extra)
    first[0].start()
    own[0] = part(core, 0)
    for j in range(count):
        if j + 1 < count:
            near_out[j + 1] = part(1 - core, j + 1).astype(jnp.bfloat16)
            first[j + 1].start()
            own[j + 1] = part(core, j + 1)
        elif beside is not None:
            beside()
        first[j].wait_recv()
        far_out[j] = (own[j] + near_in[j].astype(jnp.float32)).astype(jnp.bfloat16)
        second[j].start()
    for j in range(count):
        second[j].wait_recv()
        columns = pl.ds(pl.multiple_of(core * half + j * CHUNK, CHUNK), CHUNK)
        out_ref[:, columns] = (
            far_out[j].astype(jnp.float32) + far_in[j].astype(jnp.float32)
        ).astype(jnp.bfloat16)
        third[j].start()
    for j in range(count):
        first[j].wait_send()
        second[j].wait_send()
        third[j].wait()


def group_total(x, w, transposed, collective_id):
    rows = x.shape[0]
    columns = w.shape[0] if transposed else w.shape[1]
    count = columns // 2 // CHUNK
    vmem = pl.BlockSpec(memory_space=pltpu.VMEM)
    slot = pltpu.VMEM((count, rows, CHUNK), jnp.bfloat16)
    return pl.pallas_call(
        functools.partial(total_kernel, transposed),
        out_shape=jax.ShapeDtypeStruct((rows, columns), jnp.bfloat16),
        in_specs=[vmem, vmem],
        out_specs=vmem,
        scratch_shapes=[pltpu.VMEM((count, rows, CHUNK), jnp.float32), slot, slot, slot, slot]
        + [pltpu.SemaphoreType.DMA((count,))] * 6,
        compiler_params=pltpu.CompilerParams(
            collective_id=collective_id, has_side_effects=True, vmem_limit_bytes=32 * 2**20
        ),
        cost_estimate=pl.CostEstimate(
            flops=2 * rows * columns * x.shape[1], bytes_accessed=rows * columns * 8, transcendentals=0
        ),
    )(x, w).astype(jnp.float32)


def bit_reverse(value, bits):
    return sum(((value >> i) & 1) << (bits - 1 - i) for i in range(bits))


def last_kernel(n, scale, blocks, x_ref, w_ref, normal_ref, vec_ref, *refs):
    grads, refs = refs[:blocks], refs[blocks:]
    out_ref, vec_out, refs = refs[0], refs[1], refs[2:]
    outs, refs = refs[:blocks], refs[blocks:]
    total_scratch, refs = refs[:11], refs[11:]
    work, refs = refs[:blocks], refs[blocks:]
    land, refs = refs[:blocks], refs[blocks:]
    vec_work, vec_land, block_send, block_recv, vec_send, vec_recv = refs
    stages = n.bit_length() - 1
    me = lax.axis_index("dp")
    bits = [lax.rem(me // 2**s, 2) for s in range(stages)]
    partners = [me + 2**s * (1 - 2 * bits[s]) for s in range(stages)]
    barrier = pltpu.get_barrier_semaphore()
    for partner in partners:
        pl.semaphore_signal(barrier, inc=1, device_id={"dp": partner}, device_id_type=MESH)

    keeps, gives, first = [], [], 0
    for s in range(stages):
        half = n >> (s + 1)
        gives.append(first + (1 - bits[s]) * half)
        first = first + bits[s] * half
        keeps.append(first)

    def block_copy(s, k):
        half = n >> (s + 1)
        return pltpu.make_async_remote_copy(
            src_ref=work[k].at[pl.ds(gives[s], half)],
            dst_ref=land[k].at[pl.ds(n - 2 * half, half)],
            send_sem=block_send.at[s, k], recv_sem=block_recv.at[s, k],
            device_id={"dp": partners[s]}, device_id_type=MESH,
        )

    def send_blocks():
        for k in range(blocks):
            for p in range(n):
                work[k][p] = grads[k][bit_reverse(p, stages)]
            block_copy(0, k).start()

    def finish(s, k):
        half = n >> (s + 1)
        block_copy(s, k).wait_recv()
        mine = pl.ds(keeps[s], half)
        summed = work[k][mine].astype(jnp.float32) + land[k][n - 2 * half : n - half].astype(jnp.float32)
        if s + 1 < stages:
            work[k][mine] = summed.astype(jnp.bfloat16)
            block_copy(s + 1, k).start()
        else:
            outs[k][...] = summed[0] * scale

    total_kernel(True, x_ref, w_ref, out_ref, *total_scratch, extra=stages, beside=send_blocks)

    total = out_ref[...].astype(jnp.float32)
    vec_work[0] = vec_ref[...]
    vec_work[0, 0:1] = jnp.sum(total * normal_ref[...], axis=0, keepdims=True)
    vec_work[0, 1:2] = jnp.sum(total, axis=0, keepdims=True)

    def vec_copy(s):
        return pltpu.make_async_remote_copy(
            src_ref=vec_work.at[s], dst_ref=vec_land.at[s], send_sem=vec_send.at[s], recv_sem=vec_recv.at[s],
            device_id={"dp": partners[s]}, device_id_type=MESH,
        )

    vec_copy(0).start()
    for wave in range(blocks + stages - 1):
        for s in range(stages):
            if 0 <= wave - s < blocks:
                finish(s, wave - s)
    for s in range(stages):
        vec_copy(s).wait_recv()
        summed = vec_work[s] + vec_land[s]
        if s + 1 < stages:
            vec_work[s + 1] = summed
            vec_copy(s + 1).start()
        else:
            vec_out[...] = summed * scale
    for s in range(stages):
        vec_copy(s).wait_send()
        for k in range(blocks):
            block_copy(s, k).wait_send()


def last_total(x, w, normal, vec, grads, scale):
    n = lax.axis_size("dp")
    stages = n.bit_length() - 1
    assert n == 2**stages
    rows, columns, count = x.shape[0], w.shape[0], w.shape[0] // 2 // CHUNK
    depth = grads[0].shape[0] // n
    held = -(-depth // 16) * 16
    grads = [jnp.pad(g.reshape(n, depth, -1), ((0, 0), (0, held - depth), (0, 0))) for g in grads]
    blocks = len(grads)
    vmem = pl.BlockSpec(memory_space=pltpu.VMEM)
    slot = pltpu.VMEM((count, rows, CHUNK), jnp.bfloat16)
    total, vec, *parts = pl.pallas_call(
        functools.partial(last_kernel, n, scale, blocks),
        out_shape=[jax.ShapeDtypeStruct((rows, columns), jnp.bfloat16), jax.ShapeDtypeStruct(vec.shape, jnp.float32)]
        + [jax.ShapeDtypeStruct(g.shape[1:], jnp.float32) for g in grads],
        in_specs=[vmem] * (4 + blocks),
        out_specs=[vmem] * (2 + blocks),
        scratch_shapes=[pltpu.VMEM((count, rows, CHUNK), jnp.float32), slot, slot, slot, slot]
        + [pltpu.SemaphoreType.DMA((count,))] * 6
        + [pltpu.VMEM(g.shape, jnp.bfloat16) for g in grads]
        + [pltpu.VMEM((n - 1,) + g.shape[1:], jnp.bfloat16) for g in grads]
        + [pltpu.VMEM((stages,) + vec.shape, jnp.float32)] * 2
        + [pltpu.SemaphoreType.DMA((stages, blocks))] * 2
        + [pltpu.SemaphoreType.DMA((stages,))] * 2,
        compiler_params=pltpu.CompilerParams(
            collective_id=4, has_side_effects=True, vmem_limit_bytes=48 * 2**20
        ),
        cost_estimate=pl.CostEstimate(flops=10**9, bytes_accessed=2 * 10**7, transcendentals=0),
    )(x, w, normal, vec, *grads)
    return total.astype(jnp.float32), vec, [part[:depth] for part in parts]


VECTORS = (0, 1, 5, 6, 7, 9, 11)
MATRICES = (10, 8, 2, 4)


def vector_rows(grads):
    width = grads[0].shape[0]
    bias = grads[3].reshape(1, -1)
    rows = [grads[i].reshape(1, -1) for i in VECTORS]
    return jnp.concatenate(rows + [jnp.pad(bias, ((0, 0), (0, width - bias.shape[1])))], axis=0)


def attend_scores(queries, key_vecs, allowed):
    score_scale = queries.shape[-1] ** (-0.5)
    scores = (
        jnp.einsum("rqhd,rkhd->rhqk", queries, key_vecs, preferred_element_type=jnp.float32)
        * score_scale
    )
    return jnp.where(allowed, scores, NEG_FILL)


def forward_layer(hidden, allowed, params, batch_rows):
    (
        gain_one,
        shift_one,
        qkv_w,
        qv_b,
        out_w,
        out_b,
        gain_two,
        shift_two,
        up_w,
        up_b,
        down_w,
        down_b,
    ) = params
    tok_count = hidden.shape[0]
    local_heads = qv_b.shape[0]
    head_size = qv_b.shape[1] // 2
    normed, normal_one, inverse_one = layer_norm(hidden, gain_one, shift_one)
    normed_b = normed.astype(jnp.bfloat16)
    projected = jnp.dot(normed_b, qkv_w, preferred_element_type=jnp.float32)
    projected = projected.reshape(batch_rows, tok_count // batch_rows, local_heads, 3, head_size)
    queries = (projected[:, :, :, 0] + qv_b[:, :head_size]).astype(jnp.bfloat16)
    key_vecs = projected[:, :, :, 1].astype(jnp.bfloat16)
    values = (projected[:, :, :, 2] + qv_b[:, head_size:]).astype(jnp.bfloat16)
    scores = attend_scores(queries, key_vecs, allowed)
    row_top = jnp.max(scores, axis=-1, keepdims=True)
    log_total = row_top + jnp.log(jnp.sum(jnp.exp(scores - row_top), axis=-1, keepdims=True))
    weights = jnp.exp(scores - log_total).astype(jnp.bfloat16)
    mixed_heads = jnp.einsum("rhqk,rkhd->rqhd", weights, values, preferred_element_type=jnp.float32)
    mixed_heads = mixed_heads.astype(jnp.bfloat16).reshape(tok_count, local_heads * head_size)
    after_attn = (
        hidden
        + group_total(mixed_heads, out_w, False, 0)
        + out_b
    )
    middle, normal_two, inverse_two = layer_norm(after_attn, gain_two, shift_two)
    mid_b = middle.astype(jnp.bfloat16)
    preact = jnp.dot(mid_b, up_w, preferred_element_type=jnp.float32) + up_b
    gelu_out, gelu_slope = gelu_pair(preact)
    gelu_b = gelu_out.astype(jnp.bfloat16)
    block_out = (
        after_attn
        + group_total(gelu_b, down_w, False, 1)
        + down_b
    )
    saved = (
        normed_b,
        normal_one,
        inverse_one,
        queries,
        key_vecs,
        values,
        log_total,
        mixed_heads,
        normal_two,
        inverse_two,
        mid_b,
        gelu_slope,
        gelu_b,
    )
    return (block_out, saved)


def backward_layer(grad_out, allowed, params, saved, batch_rows, later=None, scale=None):
    (
        gain_one,
        shift_one,
        qkv_w,
        qv_b,
        out_w,
        out_b,
        gain_two,
        shift_two,
        up_w,
        up_b,
        down_w,
        down_b,
    ) = params
    (
        normed_b,
        normal_one,
        inverse_one,
        queries,
        key_vecs,
        values,
        log_total,
        mixed_heads,
        normal_two,
        inverse_two,
        mid_b,
        gelu_slope,
        gelu_b,
    ) = saved
    tok_count = grad_out.shape[0]
    local_heads = qv_b.shape[0]
    head_size = qv_b.shape[1] // 2
    score_scale = head_size ** (-0.5)
    down_b_grad = jnp.sum(grad_out, axis=0)
    grad_out_b = grad_out.astype(jnp.bfloat16)
    down_w_grad = jnp.einsum("nd,nf->df", grad_out_b, gelu_b, preferred_element_type=jnp.float32)
    gelu_grad = jnp.einsum("nd,fd->nf", grad_out_b, down_w, preferred_element_type=jnp.float32)
    pre_grad = gelu_grad * gelu_slope
    up_b_grad = jnp.sum(pre_grad, axis=0)
    pre_grad_b = pre_grad.astype(jnp.bfloat16)
    up_w_grad = jnp.einsum("nd,nf->df", mid_b, pre_grad_b, preferred_element_type=jnp.float32)
    mid_grad = group_total(pre_grad_b, up_w, True, 2)
    gain_two_grad = jnp.sum(mid_grad * normal_two, axis=0)
    shift_two_grad = jnp.sum(mid_grad, axis=0)
    resid_grad = grad_out + norm_backward(mid_grad, normal_two, inverse_two, gain_two)
    out_b_grad = jnp.sum(resid_grad, axis=0)
    resid_b = resid_grad.astype(jnp.bfloat16)
    out_w_grad = jnp.einsum("nd,nk->dk", resid_b, mixed_heads, preferred_element_type=jnp.float32)
    heads_grad = jnp.einsum("nd,kd->nk", resid_b, out_w, preferred_element_type=jnp.float32).astype(
        jnp.bfloat16
    )
    heads_grad = heads_grad.reshape(batch_rows, tok_count // batch_rows, local_heads, head_size)
    scores = attend_scores(queries, key_vecs, allowed)
    probs = jnp.exp(scores - log_total)
    probs_b = probs.astype(jnp.bfloat16)
    prob_grad = jnp.einsum(
        "rqhd,rkhd->rhqk", heads_grad, values, preferred_element_type=jnp.float32
    )
    mixed_four = mixed_heads.reshape(batch_rows, tok_count // batch_rows, local_heads, head_size)
    row_dots = jnp.sum(heads_grad.astype(jnp.float32) * mixed_four.astype(jnp.float32), axis=-1)
    row_dots = jnp.transpose(row_dots, (0, 2, 1))[..., None]
    score_grad = (probs * (prob_grad - row_dots) * score_scale).astype(jnp.bfloat16)
    query_grad = jnp.einsum(
        "rhqk,rkhd->rqhd", score_grad, key_vecs, preferred_element_type=jnp.float32
    )
    key_grad = jnp.einsum(
        "rhqk,rqhd->rkhd", score_grad, queries, preferred_element_type=jnp.float32
    )
    value_grad = jnp.einsum(
        "rhqk,rqhd->rkhd", probs_b, heads_grad, preferred_element_type=jnp.float32
    )
    qv_b_grad = jnp.concatenate(
        [jnp.sum(query_grad, axis=(0, 1)), jnp.sum(value_grad, axis=(0, 1))], axis=-1
    )
    proj_grad = jnp.stack([query_grad, key_grad, value_grad], axis=3).astype(jnp.bfloat16)
    proj_grad = proj_grad.reshape(tok_count, local_heads * 3 * head_size)
    qkv_w_grad = jnp.einsum("nd,nc->dc", normed_b, proj_grad, preferred_element_type=jnp.float32)
    if later is None:
        normed_grad = group_total(proj_grad, qkv_w, True, 3)
        gain_one_grad = jnp.sum(normed_grad * normal_one, axis=0)
        shift_one_grad = jnp.sum(normed_grad, axis=0)
    else:
        gain_one_grad = shift_one_grad = jnp.zeros_like(gain_one)
    grads = (
        gain_one_grad,
        shift_one_grad,
        qkv_w_grad,
        qv_b_grad,
        out_w_grad,
        out_b_grad,
        gain_two_grad,
        shift_two_grad,
        up_w_grad,
        up_b_grad,
        down_w_grad,
        down_b_grad,
    )
    vec = vector_rows(grads)
    matrices = [grads[i].astype(jnp.bfloat16) for i in MATRICES]
    if later is not None:
        vec = jnp.concatenate([vec, later], axis=0)
        normed_grad, vec, matrices = last_total(proj_grad, qkv_w, normal_one, vec, matrices, scale)
    input_grad = resid_grad + norm_backward(normed_grad, normal_one, inverse_one, gain_one)
    return (input_grad, vec, matrices)


def body(
    tokens,
    segment_ids,
    norm1_gain,
    norm1_shift,
    qkv_weight,
    qv_bias,
    out_weight,
    out_bias,
    norm2_gain,
    norm2_shift,
    fc1_weight,
    fc1_bias,
    fc2_weight,
    fc2_bias,
    cotangent,
):
    stacked = (
        norm1_gain,
        norm1_shift,
        qkv_weight,
        qv_bias,
        out_weight,
        out_bias,
        norm2_gain,
        norm2_shift,
        fc1_weight,
        fc1_bias,
        fc2_weight,
        fc2_bias,
    )
    batch_rows, seq_len = segment_ids.shape
    layer_count = norm1_gain.shape[0]
    grad_scale = float(batch_rows * seq_len * lax.axis_size("dp")) ** (-0.5)
    padded = -(-seq_len // 16) * 16
    extra = padded - seq_len
    segment_ids = jnp.pad(segment_ids, ((0, 0), (0, extra)), constant_values=-1)
    same_doc = segment_ids[:, :, None] == segment_ids[:, None, :]
    positions = lax.broadcasted_iota(jnp.int32, (padded, padded), 0)
    earlier = lax.broadcasted_iota(jnp.int32, (padded, padded), 1) <= positions
    allowed = (same_doc & earlier[None])[:, None]

    def widen(rows):
        rows = rows.astype(jnp.float32).reshape(batch_rows, seq_len, -1)
        return jnp.pad(rows, ((0, 0), (0, extra), (0, 0))).reshape(batch_rows * padded, -1)

    def narrow(rows):
        return rows.reshape(batch_rows, padded, -1)[:, :seq_len].reshape(batch_rows * seq_len, -1)

    hidden = widen(tokens)
    saved_list = []
    for layer_idx in range(layer_count):
        params = tuple((member[layer_idx] for member in stacked))
        hidden, saved = forward_layer(hidden, allowed, params, batch_rows)
        saved_list.append(saved)
    grad_flow = widen(cotangent)
    n = lax.axis_size("dp")
    depth = hidden.shape[1] // n
    later_vec = None
    matrix_parts = [None] * layer_count
    for layer_idx in reversed(range(layer_count)):
        params = tuple((member[layer_idx] for member in stacked))
        grad_flow, vec, matrices = backward_layer(
            grad_flow, allowed, params, saved_list[layer_idx], batch_rows,
            later_vec if layer_idx == 0 else None, grad_scale,
        )
        if layer_idx:
            packed = jnp.concatenate(matrices, axis=1)
            packed, grad_flow = lax.optimization_barrier((packed, grad_flow))
            later_vec = vec if later_vec is None else jnp.concatenate([vec, later_vec], axis=0)
            part = lax.psum_scatter(packed, "dp", scatter_dimension=0, tiled=True).astype(jnp.float32) * grad_scale
            widths = [m.shape[1] for m in matrices]
            ends = [sum(widths[: i + 1]) for i in range(len(widths))]
            matrix_parts[layer_idx] = [part[:, end - w : end] for w, end in zip(widths, ends)]
        else:
            matrix_parts[0] = matrices
    here = lax.axis_index("dp")
    rows = vec.reshape(layer_count, len(VECTORS) + 1, -1)
    own = lax.dynamic_slice_in_dim(rows[:, :-1], here * depth, depth, 2)
    totals = [None] * 12
    for i, position in enumerate(VECTORS):
        totals[position] = own[:, i]
    heads, features = qv_bias.shape[1:]
    bias = rows[:, -1, : heads * features].reshape(layer_count, heads, features)
    totals[3] = lax.dynamic_slice_in_dim(bias, here * (features // n), features // n, 2)
    for i, position in enumerate(MATRICES):
        member = jnp.stack([part[i] for part in matrix_parts], axis=0)
        totals[position] = jnp.swapaxes(member, 1, 2) if position in (4, 10) else member
    totals = tuple(totals)
    return (narrow(hidden), narrow(grad_flow)) + totals


def solution(mesh):
    return jax.shard_map(
        body,
        mesh=mesh,
        in_specs=(
            P("dp", None),
            P("dp", None),
            P(),
            P(),
            P(None, None, "tensor"),
            P(None, "tensor", None),
            P(None, "tensor", None),
            P(),
            P(),
            P(),
            P(None, None, "tensor"),
            P(None, "tensor"),
            P(None, "tensor", None),
            P(),
            P("dp", None),
        ),
        out_specs=(
            P("dp", None),
            P("dp", None),
            P(None, "dp"),
            P(None, "dp"),
            P(None, "dp", "tensor"),
            P(None, "tensor", "dp"),
            P(None, "tensor", "dp"),
            P(None, "dp"),
            P(None, "dp"),
            P(None, "dp"),
            P(None, "dp", "tensor"),
            P(None, ("tensor", "dp")),
            P(None, "tensor", "dp"),
            P(None, "dp"),
        ),
        check_vma=False,
    )
```

```python
import functools

import jax
import jax.numpy as jnp
from jax import lax
from jax.experimental import pallas as pl
from jax.experimental.pallas import tpu as pltpu
from jax.sharding import PartitionSpec as P

NORM_EPS = 1e-05
GELU_C = 0.7978845608028654
NEG_FILL = -1e30


def layer_norm(hidden, norm_gain, norm_shift):
    row_mean = jnp.mean(hidden, axis=-1, keepdims=True)
    centred = hidden - row_mean
    variance = jnp.mean(centred * centred, axis=-1, keepdims=True)
    inverse = lax.rsqrt(variance + NORM_EPS)
    normal = centred * inverse
    return (normal * norm_gain + norm_shift, normal, inverse)


def norm_backward(grad_out, normal, inverse, norm_gain):
    scaled = grad_out * norm_gain
    return inverse * (
        scaled
        - jnp.mean(scaled, axis=-1, keepdims=True)
        - normal * jnp.mean(scaled * normal, axis=-1, keepdims=True)
    )


def gelu_pair(preact):
    inner_arg = GELU_C * (preact + 0.044715 * preact * preact * preact)
    tanh_value = jnp.tanh(inner_arg)
    gelu_out = 0.5 * preact * (1.0 + tanh_value)
    gelu_slope = 0.5 * (1.0 + tanh_value) + 0.5 * preact * (
        1.0 - tanh_value * tanh_value
    ) * GELU_C * (1.0 + 3.0 * 0.044715 * preact * preact)
    return (gelu_out, gelu_slope)


MESH = pl.DeviceIdType.MESH
CHUNK = 128


def total_kernel(transposed, x_ref, w_ref, out_ref, own, near_out, near_in, far_out, far_in,
                 near_send, near_recv, far_send, far_recv, back_send, back_recv, extra=0, beside=None):
    here = lax.axis_index("tensor")
    core = lax.rem(here, 2)
    near = here + 1 - 2 * core
    far = lax.rem(here + 2, 4)
    barrier = pltpu.get_barrier_semaphore()
    for other in (near, far):
        pl.semaphore_signal(barrier, inc=1, device_id={"tensor": other}, device_id_type=MESH)

    half = out_ref.shape[1] // 2
    count = half // CHUNK

    def part(side, j):
        start = pl.multiple_of(side * half + j * CHUNK, CHUNK)
        if transposed:
            return lax.dot_general(
                x_ref[...], w_ref[pl.ds(start, CHUNK), :], (((1,), (1,)), ((), ())),
                preferred_element_type=jnp.float32,
            )
        return jnp.dot(x_ref[...], w_ref[:, pl.ds(start, CHUNK)], preferred_element_type=jnp.float32)

    def copy(src, dst, send, recv, other):
        return pltpu.make_async_remote_copy(
            src_ref=src, dst_ref=dst, send_sem=send, recv_sem=recv,
            device_id={"tensor": other}, device_id_type=MESH,
        )

    first = [copy(near_out.at[j], near_in.at[j], near_send.at[j], near_recv.at[j], near) for j in range(count)]
    second = [copy(far_out.at[j], far_in.at[j], far_send.at[j], far_recv.at[j], far) for j in range(count)]

    def back_copy(j):
        columns = pl.ds(pl.multiple_of(core * half + j * CHUNK, CHUNK), CHUNK)
        return copy(out_ref.at[:, columns], out_ref.at[:, columns], back_send.at[j], back_recv.at[j], near)

    third = [back_copy(j) for j in range(count)]

    near_out[0] = part(1 - core, 0).astype(jnp.bfloat16)
    pl.semaphore_wait(barrier, 2 + extra)
    first[0].start()
    own[0] = part(core, 0)
    for j in range(count):
        if j + 1 < count:
            near_out[j + 1] = part(1 - core, j + 1).astype(jnp.bfloat16)
            first[j + 1].start()
            own[j + 1] = part(core, j + 1)
        elif beside is not None:
            beside()
        first[j].wait_recv()
        far_out[j] = (own[j] + near_in[j].astype(jnp.float32)).astype(jnp.bfloat16)
        second[j].start()
    for j in range(count):
        second[j].wait_recv()
        columns = pl.ds(pl.multiple_of(core * half + j * CHUNK, CHUNK), CHUNK)
        out_ref[:, columns] = (
            far_out[j].astype(jnp.float32) + far_in[j].astype(jnp.float32)
        ).astype(jnp.bfloat16)
        third[j].start()
    for j in range(count):
        first[j].wait_send()
        second[j].wait_send()
        third[j].wait()


def group_total(x, w, transposed, collective_id):
    rows = x.shape[0]
    columns = w.shape[0] if transposed else w.shape[1]
    count = columns // 2 // CHUNK
    vmem = pl.BlockSpec(memory_space=pltpu.VMEM)
    slot = pltpu.VMEM((count, rows, CHUNK), jnp.bfloat16)
    return pl.pallas_call(
        functools.partial(total_kernel, transposed),
        out_shape=jax.ShapeDtypeStruct((rows, columns), jnp.bfloat16),
        in_specs=[vmem, vmem],
        out_specs=vmem,
        scratch_shapes=[pltpu.VMEM((count, rows, CHUNK), jnp.float32), slot, slot, slot, slot]
        + [pltpu.SemaphoreType.DMA((count,))] * 6,
        compiler_params=pltpu.CompilerParams(
            collective_id=collective_id, has_side_effects=True, vmem_limit_bytes=32 * 2**20
        ),
        cost_estimate=pl.CostEstimate(
            flops=2 * rows * columns * x.shape[1], bytes_accessed=rows * columns * 8, transcendentals=0
        ),
    )(x, w).astype(jnp.float32)


def slab_at(place, order):
    last = len(order) - 1
    return sum(((place >> (last - j)) & 1) << bit for j, bit in enumerate(order))


def bit_order(stages, k):
    order = list(range(stages))
    if k == 2 and stages > 1:
        order[:2] = [1, 0]
    return order


def last_kernel(n, scale, blocks, x_ref, w_ref, normal_ref, vec_ref, *refs):
    grads, refs = refs[:blocks], refs[blocks:]
    out_ref, vec_out, refs = refs[0], refs[1], refs[2:]
    outs, refs = refs[:blocks], refs[blocks:]
    total_scratch, refs = refs[:11], refs[11:]
    work, refs = refs[:blocks], refs[blocks:]
    land, refs = refs[:blocks], refs[blocks:]
    vec_work, vec_land, block_send, block_recv, vec_send, vec_recv = refs
    stages = n.bit_length() - 1
    me = lax.axis_index("dp")
    bits = [lax.rem(me // 2**s, 2) for s in range(stages)]
    partners = [me + 2**s * (1 - 2 * bits[s]) for s in range(stages)]
    barrier = pltpu.get_barrier_semaphore()
    for partner in partners:
        pl.semaphore_signal(barrier, inc=1, device_id={"dp": partner}, device_id_type=MESH)

    orders = [bit_order(stages, k) for k in range(blocks)]
    keeps, gives = {}, {}
    for k in range(blocks):
        first = 0
        for s in range(stages):
            half, bit = n >> (s + 1), bits[orders[k][s]]
            gives[s, k] = first + (1 - bit) * half
            first = first + bit * half
            keeps[s, k] = first

    def block_copy(s, k):
        half = n >> (s + 1)
        return pltpu.make_async_remote_copy(
            src_ref=work[k].at[pl.ds(gives[s, k], half)],
            dst_ref=land[k].at[pl.ds(n - 2 * half, half)],
            send_sem=block_send.at[s, k], recv_sem=block_recv.at[s, k],
            device_id={"dp": partners[orders[k][s]]}, device_id_type=MESH,
        )

    def send_blocks():
        for k in sorted(range(blocks), key=lambda k: orders[k][0] == 0):
            for p in range(n):
                work[k][p] = grads[k][slab_at(p, orders[k])]
            block_copy(0, k).start()

    def finish(s, k):
        half = n >> (s + 1)
        block_copy(s, k).wait_recv()
        mine = pl.ds(keeps[s, k], half)
        summed = work[k][mine].astype(jnp.float32) + land[k][n - 2 * half : n - half].astype(jnp.float32)
        if s + 1 < stages:
            work[k][mine] = summed.astype(jnp.bfloat16)
            block_copy(s + 1, k).start()
        else:
            outs[k][...] = summed[0] * scale

    total_kernel(True, x_ref, w_ref, out_ref, *total_scratch, extra=stages, beside=send_blocks)

    total = out_ref[...].astype(jnp.float32)
    vec_work[0] = vec_ref[...]
    vec_work[0, 0:1] = jnp.sum(total * normal_ref[...], axis=0, keepdims=True)
    vec_work[0, 1:2] = jnp.sum(total, axis=0, keepdims=True)

    def vec_copy(s):
        return pltpu.make_async_remote_copy(
            src_ref=vec_work.at[s], dst_ref=vec_land.at[s], send_sem=vec_send.at[s], recv_sem=vec_recv.at[s],
            device_id={"dp": partners[s]}, device_id_type=MESH,
        )

    vec_copy(0).start()
    for wave in range(blocks + stages - 1):
        for s in range(stages):
            if 0 <= wave - s < blocks:
                finish(s, wave - s)
    for s in range(stages):
        vec_copy(s).wait_recv()
        summed = vec_work[s] + vec_land[s]
        if s + 1 < stages:
            vec_work[s + 1] = summed
            vec_copy(s + 1).start()
        else:
            vec_out[...] = summed * scale
    for s in range(stages):
        vec_copy(s).wait_send()
        for k in range(blocks):
            block_copy(s, k).wait_send()


def last_total(x, w, normal, vec, grads, scale):
    n = lax.axis_size("dp")
    stages = n.bit_length() - 1
    assert n == 2**stages
    rows, columns, count = x.shape[0], w.shape[0], w.shape[0] // 2 // CHUNK
    depth = grads[0].shape[0] // n
    held = -(-depth // 16) * 16
    grads = [jnp.pad(g.reshape(n, depth, -1), ((0, 0), (0, held - depth), (0, 0))) for g in grads]
    blocks = len(grads)
    vmem = pl.BlockSpec(memory_space=pltpu.VMEM)
    slot = pltpu.VMEM((count, rows, CHUNK), jnp.bfloat16)
    total, vec, *parts = pl.pallas_call(
        functools.partial(last_kernel, n, scale, blocks),
        out_shape=[jax.ShapeDtypeStruct((rows, columns), jnp.bfloat16), jax.ShapeDtypeStruct(vec.shape, jnp.float32)]
        + [jax.ShapeDtypeStruct(g.shape[1:], jnp.float32) for g in grads],
        in_specs=[vmem] * (4 + blocks),
        out_specs=[vmem] * (2 + blocks),
        scratch_shapes=[pltpu.VMEM((count, rows, CHUNK), jnp.float32), slot, slot, slot, slot]
        + [pltpu.SemaphoreType.DMA((count,))] * 6
        + [pltpu.VMEM(g.shape, jnp.bfloat16) for g in grads]
        + [pltpu.VMEM((n - 1,) + g.shape[1:], jnp.bfloat16) for g in grads]
        + [pltpu.VMEM((stages,) + vec.shape, jnp.float32)] * 2
        + [pltpu.SemaphoreType.DMA((stages, blocks))] * 2
        + [pltpu.SemaphoreType.DMA((stages,))] * 2,
        compiler_params=pltpu.CompilerParams(
            collective_id=4, has_side_effects=True, vmem_limit_bytes=48 * 2**20
        ),
        cost_estimate=pl.CostEstimate(flops=10**9, bytes_accessed=2 * 10**7, transcendentals=0),
    )(x, w, normal, vec, *grads)
    return total.astype(jnp.float32), vec, [part[:depth] for part in parts]


VECTORS = (0, 1, 5, 6, 7, 9, 11)
MATRICES = (10, 8, 2, 4)


def vector_rows(grads):
    width = grads[0].shape[0]
    bias = grads[3].reshape(1, -1)
    rows = [grads[i].reshape(1, -1) for i in VECTORS]
    return jnp.concatenate(rows + [jnp.pad(bias, ((0, 0), (0, width - bias.shape[1])))], axis=0)


def attend_scores(queries, key_vecs, allowed):
    score_scale = queries.shape[-1] ** (-0.5)
    scores = (
        jnp.einsum("rqhd,rkhd->rhqk", queries, key_vecs, preferred_element_type=jnp.float32)
        * score_scale
    )
    return jnp.where(allowed, scores, NEG_FILL)


def forward_layer(hidden, allowed, params, batch_rows):
    (
        gain_one,
        shift_one,
        qkv_w,
        qv_b,
        out_w,
        out_b,
        gain_two,
        shift_two,
        up_w,
        up_b,
        down_w,
        down_b,
    ) = params
    tok_count = hidden.shape[0]
    local_heads = qv_b.shape[0]
    head_size = qv_b.shape[1] // 2
    normed, normal_one, inverse_one = layer_norm(hidden, gain_one, shift_one)
    normed_b = normed.astype(jnp.bfloat16)
    projected = jnp.dot(normed_b, qkv_w, preferred_element_type=jnp.float32)
    projected = projected.reshape(batch_rows, tok_count // batch_rows, local_heads, 3, head_size)
    queries = (projected[:, :, :, 0] + qv_b[:, :head_size]).astype(jnp.bfloat16)
    key_vecs = projected[:, :, :, 1].astype(jnp.bfloat16)
    values = (projected[:, :, :, 2] + qv_b[:, head_size:]).astype(jnp.bfloat16)
    scores = attend_scores(queries, key_vecs, allowed)
    row_top = jnp.max(scores, axis=-1, keepdims=True)
    log_total = row_top + jnp.log(jnp.sum(jnp.exp(scores - row_top), axis=-1, keepdims=True))
    weights = jnp.exp(scores - log_total).astype(jnp.bfloat16)
    mixed_heads = jnp.einsum("rhqk,rkhd->rqhd", weights, values, preferred_element_type=jnp.float32)
    mixed_heads = mixed_heads.astype(jnp.bfloat16).reshape(tok_count, local_heads * head_size)
    after_attn = (
        hidden
        + group_total(mixed_heads, out_w, False, 0)
        + out_b
    )
    middle, normal_two, inverse_two = layer_norm(after_attn, gain_two, shift_two)
    mid_b = middle.astype(jnp.bfloat16)
    preact = jnp.dot(mid_b, up_w, preferred_element_type=jnp.float32) + up_b
    gelu_out, gelu_slope = gelu_pair(preact)
    gelu_b = gelu_out.astype(jnp.bfloat16)
    block_out = (
        after_attn
        + group_total(gelu_b, down_w, False, 1)
        + down_b
    )
    saved = (
        normed_b,
        normal_one,
        inverse_one,
        queries,
        key_vecs,
        values,
        log_total,
        mixed_heads,
        normal_two,
        inverse_two,
        mid_b,
        gelu_slope,
        gelu_b,
    )
    return (block_out, saved)


def backward_layer(grad_out, allowed, params, saved, batch_rows, later=None, scale=None):
    (
        gain_one,
        shift_one,
        qkv_w,
        qv_b,
        out_w,
        out_b,
        gain_two,
        shift_two,
        up_w,
        up_b,
        down_w,
        down_b,
    ) = params
    (
        normed_b,
        normal_one,
        inverse_one,
        queries,
        key_vecs,
        values,
        log_total,
        mixed_heads,
        normal_two,
        inverse_two,
        mid_b,
        gelu_slope,
        gelu_b,
    ) = saved
    tok_count = grad_out.shape[0]
    local_heads = qv_b.shape[0]
    head_size = qv_b.shape[1] // 2
    score_scale = head_size ** (-0.5)
    down_b_grad = jnp.sum(grad_out, axis=0)
    grad_out_b = grad_out.astype(jnp.bfloat16)
    down_w_grad = jnp.einsum("nd,nf->df", grad_out_b, gelu_b, preferred_element_type=jnp.float32)
    gelu_grad = jnp.einsum("nd,fd->nf", grad_out_b, down_w, preferred_element_type=jnp.float32)
    pre_grad = gelu_grad * gelu_slope
    up_b_grad = jnp.sum(pre_grad, axis=0)
    pre_grad_b = pre_grad.astype(jnp.bfloat16)
    up_w_grad = jnp.einsum("nd,nf->df", mid_b, pre_grad_b, preferred_element_type=jnp.float32)
    mid_grad = group_total(pre_grad_b, up_w, True, 2)
    gain_two_grad = jnp.sum(mid_grad * normal_two, axis=0)
    shift_two_grad = jnp.sum(mid_grad, axis=0)
    resid_grad = grad_out + norm_backward(mid_grad, normal_two, inverse_two, gain_two)
    out_b_grad = jnp.sum(resid_grad, axis=0)
    resid_b = resid_grad.astype(jnp.bfloat16)
    out_w_grad = jnp.einsum("nd,nk->dk", resid_b, mixed_heads, preferred_element_type=jnp.float32)
    heads_grad = jnp.einsum("nd,kd->nk", resid_b, out_w, preferred_element_type=jnp.float32).astype(
        jnp.bfloat16
    )
    heads_grad = heads_grad.reshape(batch_rows, tok_count // batch_rows, local_heads, head_size)
    scores = attend_scores(queries, key_vecs, allowed)
    probs = jnp.exp(scores - log_total)
    probs_b = probs.astype(jnp.bfloat16)
    prob_grad = jnp.einsum(
        "rqhd,rkhd->rhqk", heads_grad, values, preferred_element_type=jnp.float32
    )
    mixed_four = mixed_heads.reshape(batch_rows, tok_count // batch_rows, local_heads, head_size)
    row_dots = jnp.sum(heads_grad.astype(jnp.float32) * mixed_four.astype(jnp.float32), axis=-1)
    row_dots = jnp.transpose(row_dots, (0, 2, 1))[..., None]
    score_grad = (probs * (prob_grad - row_dots) * score_scale).astype(jnp.bfloat16)
    query_grad = jnp.einsum(
        "rhqk,rkhd->rqhd", score_grad, key_vecs, preferred_element_type=jnp.float32
    )
    key_grad = jnp.einsum(
        "rhqk,rqhd->rkhd", score_grad, queries, preferred_element_type=jnp.float32
    )
    value_grad = jnp.einsum(
        "rhqk,rqhd->rkhd", probs_b, heads_grad, preferred_element_type=jnp.float32
    )
    qv_b_grad = jnp.concatenate(
        [jnp.sum(query_grad, axis=(0, 1)), jnp.sum(value_grad, axis=(0, 1))], axis=-1
    )
    proj_grad = jnp.stack([query_grad, key_grad, value_grad], axis=3).astype(jnp.bfloat16)
    proj_grad = proj_grad.reshape(tok_count, local_heads * 3 * head_size)
    qkv_w_grad = jnp.einsum("nd,nc->dc", normed_b, proj_grad, preferred_element_type=jnp.float32)
    if later is None:
        normed_grad = group_total(proj_grad, qkv_w, True, 3)
        gain_one_grad = jnp.sum(normed_grad * normal_one, axis=0)
        shift_one_grad = jnp.sum(normed_grad, axis=0)
    else:
        gain_one_grad = shift_one_grad = jnp.zeros_like(gain_one)
    grads = (
        gain_one_grad,
        shift_one_grad,
        qkv_w_grad,
        qv_b_grad,
        out_w_grad,
        out_b_grad,
        gain_two_grad,
        shift_two_grad,
        up_w_grad,
        up_b_grad,
        down_w_grad,
        down_b_grad,
    )
    vec = vector_rows(grads)
    matrices = [grads[i].astype(jnp.bfloat16) for i in MATRICES]
    if later is not None:
        vec = jnp.concatenate([vec, later], axis=0)
        normed_grad, vec, matrices = last_total(proj_grad, qkv_w, normal_one, vec, matrices, scale)
    input_grad = resid_grad + norm_backward(normed_grad, normal_one, inverse_one, gain_one)
    return (input_grad, vec, matrices)


def body(
    tokens,
    segment_ids,
    norm1_gain,
    norm1_shift,
    qkv_weight,
    qv_bias,
    out_weight,
    out_bias,
    norm2_gain,
    norm2_shift,
    fc1_weight,
    fc1_bias,
    fc2_weight,
    fc2_bias,
    cotangent,
):
    stacked = (
        norm1_gain,
        norm1_shift,
        qkv_weight,
        qv_bias,
        out_weight,
        out_bias,
        norm2_gain,
        norm2_shift,
        fc1_weight,
        fc1_bias,
        fc2_weight,
        fc2_bias,
    )
    batch_rows, seq_len = segment_ids.shape
    layer_count = norm1_gain.shape[0]
    grad_scale = float(batch_rows * seq_len * lax.axis_size("dp")) ** (-0.5)
    padded = -(-seq_len // 16) * 16
    extra = padded - seq_len
    segment_ids = jnp.pad(segment_ids, ((0, 0), (0, extra)), constant_values=-1)
    same_doc = segment_ids[:, :, None] == segment_ids[:, None, :]
    positions = lax.broadcasted_iota(jnp.int32, (padded, padded), 0)
    earlier = lax.broadcasted_iota(jnp.int32, (padded, padded), 1) <= positions
    allowed = (same_doc & earlier[None])[:, None]

    def widen(rows):
        rows = rows.astype(jnp.float32).reshape(batch_rows, seq_len, -1)
        return jnp.pad(rows, ((0, 0), (0, extra), (0, 0))).reshape(batch_rows * padded, -1)

    def narrow(rows):
        return rows.reshape(batch_rows, padded, -1)[:, :seq_len].reshape(batch_rows * seq_len, -1)

    hidden = widen(tokens)
    saved_list = []
    for layer_idx in range(layer_count):
        params = tuple((member[layer_idx] for member in stacked))
        hidden, saved = forward_layer(hidden, allowed, params, batch_rows)
        saved_list.append(saved)
    grad_flow = widen(cotangent)
    n = lax.axis_size("dp")
    depth = hidden.shape[1] // n
    later_vec = None
    matrix_parts = [None] * layer_count
    for layer_idx in reversed(range(layer_count)):
        params = tuple((member[layer_idx] for member in stacked))
        grad_flow, vec, matrices = backward_layer(
            grad_flow, allowed, params, saved_list[layer_idx], batch_rows,
            later_vec if layer_idx == 0 else None, grad_scale,
        )
        if layer_idx:
            packed = jnp.concatenate(matrices, axis=1)
            packed, grad_flow = lax.optimization_barrier((packed, grad_flow))
            later_vec = vec if later_vec is None else jnp.concatenate([vec, later_vec], axis=0)
            part = lax.psum_scatter(packed, "dp", scatter_dimension=0, tiled=True).astype(jnp.float32) * grad_scale
            widths = [m.shape[1] for m in matrices]
            ends = [sum(widths[: i + 1]) for i in range(len(widths))]
            matrix_parts[layer_idx] = [part[:, end - w : end] for w, end in zip(widths, ends)]
        else:
            matrix_parts[0] = matrices
    here = lax.axis_index("dp")
    rows = vec.reshape(layer_count, len(VECTORS) + 1, -1)
    own = lax.dynamic_slice_in_dim(rows[:, :-1], here * depth, depth, 2)
    totals = [None] * 12
    for i, position in enumerate(VECTORS):
        totals[position] = own[:, i]
    heads, features = qv_bias.shape[1:]
    bias = rows[:, -1, : heads * features].reshape(layer_count, heads, features)
    totals[3] = lax.dynamic_slice_in_dim(bias, here * (features // n), features // n, 2)
    for i, position in enumerate(MATRICES):
        member = jnp.stack([part[i] for part in matrix_parts], axis=0)
        totals[position] = jnp.swapaxes(member, 1, 2) if position in (4, 10) else member
    totals = tuple(totals)
    return (narrow(hidden), narrow(grad_flow)) + totals


def solution(mesh):
    return jax.shard_map(
        body,
        mesh=mesh,
        in_specs=(
            P("dp", None),
            P("dp", None),
            P(),
            P(),
            P(None, None, "tensor"),
            P(None, "tensor", None),
            P(None, "tensor", None),
            P(),
            P(),
            P(),
            P(None, None, "tensor"),
            P(None, "tensor"),
            P(None, "tensor", None),
            P(),
            P("dp", None),
        ),
        out_specs=(
            P("dp", None),
            P("dp", None),
            P(None, "dp"),
            P(None, "dp"),
            P(None, "dp", "tensor"),
            P(None, "tensor", "dp"),
            P(None, "tensor", "dp"),
            P(None, "dp"),
            P(None, "dp"),
            P(None, "dp"),
            P(None, "dp", "tensor"),
            P(None, ("tensor", "dp")),
            P(None, "tensor", "dp"),
            P(None, "dp"),
        ),
        check_vma=False,
    )
```
